256 devices in a mesh: mem: 16 (over y, x), lat: 16 (over z, core).
Axes of the slice: x: 4, y: 4, z: 8, core: 2. Of those that a mesh axis runs over, the one named last changes fastest.
Arguments:
- prior_sample: bfloat16 [64, 83, 131072], P('mem', None, 'lat'), may hold values from -6 to 6
- measured_values: bfloat16 [65536], P('lat'), may hold values from -8 to 8
- measured_quantity: int32 [65536], P('lat'), may hold values from 0 to 82
- measured_vertical: int32 [65536], P('lat'), may hold values from 0 to 8191
- measure_position_matrix: int32 [512, 8192], P('mem', 'lat'), may hold values from 0 to 6143, as said below
- alive_slot_number: int32 [512, 16], P('mem', 'lat'), may hold values from 1 to 512, as said below
- tapered_precision_factor: float32 [512, 8192], P('mem', 'lat'), may hold values from 0.02 to 0.5
Outputs:
- analysis: bfloat16 [64, 83, 131072], P('mem', None, 'lat')
The draws below stay inside these ranges and needn't reach their ends.
Inputs may be any that keep to these rules, and one draw needn't show every extreme that they name: `measure_position_matrix`: within a patch the indices are distinct and lie within 1024 consecutive window entries; patches of the first band never index below 1024, patches of the last band never index 5120 or above. `alive_slot_number`: every device holds a patch with exactly 512 live slots.
All inputs are finite; a program needn't handle non-finite values.
Results may differ from the reference program's by a relative error of at most 0.0046.
Values may be sent and summed in bfloat16 or wider, within the bound.
A program may use at most 128 MiB of HBM per device.

```python
import math
import jax
import jax.numpy as jnp
from jax import lax

SAMPLE_SIZE = 64
FIELD_QUANTITY = 83
L = 512
NS_STEPS = 8
PPD = 32
NOBS_DEV = 4096
HALO = 1024
PATCHES = 512
CB = 8192
MESH_VERTICALS = 131072
NOBS_T = 65536
N_MEM = 16
N_LAT = 16


def draw_measure_position_matrix(key, part):
    key = jax.random.fold_in(key, 11)
    nrows = N_MEM * PPD
    window = NOBS_DEV + 2 * HALO
    span = 2 * L
    active_strip = jnp.arange(N_LAT, dtype=jnp.int32)[:, None]
    lowest = jnp.where(active_strip == 0, HALO, 0)
    highest = jnp.where(active_strip == N_LAT - 1, HALO + NOBS_DEV - span, window - span)
    key_start, key_perm = jax.random.split(key)
    raw = jax.random.randint(key_start, (N_LAT, nrows), 0, 1 << 20, dtype=jnp.int32)
    start = lowest + raw % (highest - lowest + 1)
    keys = jax.random.split(key_perm, N_LAT * nrows)
    picks = jax.vmap(lambda one_key: jax.random.permutation(one_key, span)[:L])(keys)
    picks = picks.reshape(N_LAT, nrows, L).astype(jnp.int32)
    index = start[:, :, None] + picks
    return jnp.transpose(index, (1, 0, 2)).reshape(nrows, N_LAT * L).astype(jnp.int32)


def draw_alive_slot_number(key, part):
    key = jax.random.fold_in(key, 12)
    key_level, key_less = jax.random.split(key)
    quarter = L // 4
    level = jax.random.randint(key_level, (N_MEM, 1, N_LAT), 1, 5, dtype=jnp.int32)
    less = jax.random.randint(key_less, (N_MEM, PPD, N_LAT), 0, quarter, dtype=jnp.int32)
    counts = jnp.maximum(level * quarter - less, 1)
    counts = jnp.minimum(counts, L)
    counts = counts.at[:, 0, :].set(L)
    return counts.reshape(N_MEM * PPD, N_LAT).astype(jnp.int32)


def place_ends(entries, key, smallest, largest):
    longest = entries.shape.index(max(entries.shape))
    spots = []
    for shift in (0, 1):
        where = [jax.random.randint(jax.random.fold_in(key, axis), (), 0, length) for axis, length in enumerate(entries.shape)]
        where[longest] = (where[longest] + shift) % entries.shape[longest]
        spots.append(tuple(where))
    return entries.at[spots[0]].set(smallest).at[spots[1]].set(largest)


def block_scale(key, dims, cuts, low, high):
    factor_of, own = 1.0, jax.random.fold_in(key, 6)
    for position, parts in cuts:
        steps = jnp.exp(jax.random.uniform(jax.random.fold_in(own, position), (parts,), jnp.float32, low / len(cuts), high / len(cuts)))
        factor_of = factor_of * jnp.repeat(steps, dims[position] // parts).reshape([-1 if axis == position else 1 for axis in range(len(dims))])
    return factor_of


def scatter_about(stream_key, dims, width, reach, cuts=(), held_as=jnp.bfloat16):
    drawn = jax.random.normal(stream_key, dims, jnp.float32) * width
    if len(cuts) > 0:
        drawn = block_scale(stream_key, dims, cuts, -0.22, 0.18) * drawn
    return jnp.clip(drawn, min=-reach, max=reach).astype(held_as)


def setup_inputs(seed: int = 0) -> dict:
    key_list = jax.random.split(jax.random.key(seed), 8)
    return {
        "prior_sample": scatter_about(key_list[0], (SAMPLE_SIZE, FIELD_QUANTITY, MESH_VERTICALS), 1.0, 6.0, ((0, 16), (2, 16))),
        "measured_values": scatter_about(key_list[1], (NOBS_T,), 1.5, 8.0, ((0, 16),)),
        "measured_quantity": place_ends(jax.random.randint(key_list[2], (NOBS_T,), 0, FIELD_QUANTITY), jax.random.fold_in(key_list[2], 1), 0, FIELD_QUANTITY - 1).astype(jnp.int32),
        "measured_vertical": place_ends(jax.random.randint(key_list[3], (NOBS_T,), 0, CB), jax.random.fold_in(key_list[3], 1), 0, CB - 1).astype(jnp.int32),
        "measure_position_matrix": draw_measure_position_matrix(jax.random.fold_in(key_list[7], 71), 0),
        "alive_slot_number": draw_alive_slot_number(jax.random.fold_in(key_list[7], 71), 0),
        "tapered_precision_factor": jnp.clip(jnp.exp(math.log(0.5) - 3.218876 * jax.random.uniform(key_list[6], (PATCHES, N_LAT * L), jnp.float32) ** block_scale(key_list[6], (PATCHES, N_LAT * L), ((0, 16), (1, 16)), -0.2, 0.2)), 0.02, 0.5),
    }


def patch_weights(pert, depart, weight, counts):
    sample_fields = pert.shape[0]
    slots = pert.shape[2]
    live = jnp.arange(slots, dtype=jnp.int32)[None, :] < counts[:, None]
    rweight = jnp.where(live, weight, jnp.zeros_like(weight))
    scaled = pert * rweight[None, :, :]
    identity = jnp.eye(sample_fields, dtype=pert.dtype)
    gram = jnp.einsum('jpl,kpl->pjk', pert, scaled, precision=lax.Precision.HIGHEST) + (sample_fields - 1.0) * identity
    trace_sum = jnp.trace(gram, axis1=1, axis2=2)
    root = gram / trace_sum[:, None, None]
    inverse = jnp.broadcast_to(identity, root.shape)
    for sweep in range(NS_STEPS):
        middle = 0.5 * (3.0 * identity - jnp.matmul(inverse, root, precision=lax.Precision.HIGHEST))
        root = jnp.matmul(root, middle, precision=lax.Precision.HIGHEST)
        inverse = jnp.matmul(middle, inverse, precision=lax.Precision.HIGHEST)
    spread = inverse * (jnp.sqrt(sample_fields - 1.0) / jnp.sqrt(trace_sum))[:, None, None]
    covar = jnp.matmul(inverse, inverse, precision=lax.Precision.HIGHEST) / trace_sum[:, None, None]
    project = jnp.einsum('jpl,pl->pj', scaled, depart, precision=lax.Precision.HIGHEST)
    shift = jnp.einsum('pjk,pk->pj', covar, project, precision=lax.Precision.HIGHEST)
    full = spread + shift[:, :, None]
    return (full + (1.0 - lax.optimization_barrier(jnp.sum(full, axis=1, keepdims=True))) / sample_fields).astype(jnp.bfloat16)

def reference(prior_sample, measured_values, measured_quantity, measured_vertical, measure_position_matrix, alive_slot_number, tapered_precision_factor):
    sample_fields, quantity_number, vertical_sum_number = prior_sample.shape
    verticals_in_strip = vertical_sum_number // N_LAT
    field_mesh = prior_sample.reshape(sample_fields, quantity_number, N_LAT, verticals_in_strip)
    owner = jnp.arange(N_LAT * NOBS_DEV, dtype=jnp.int32) // NOBS_DEV
    equiv = field_mesh[:, measured_quantity, owner, measured_vertical]
    stacked = jnp.concatenate([equiv, measured_values[None, :]], axis=0)
    padded = jnp.pad(stacked, ((0, 0), (HALO, HALO)))
    window = NOBS_DEV + 2 * HALO

    def one_band(active_strip):
        active_strip = active_strip.astype(jnp.int32)
        local = lax.dynamic_slice_in_dim(padded, active_strip * NOBS_DEV, window, 1)
        equiv_f = local[:sample_fields].astype(jnp.float32)
        mean = lax.optimization_barrier(jnp.sum(equiv_f, axis=0)) / sample_fields
        pert = equiv_f - mean[None, :]
        depart = local[sample_fields].astype(jnp.float32) - mean
        lists = lax.dynamic_slice_in_dim(measure_position_matrix, active_strip * L, L, 1)
        counts = lax.dynamic_slice_in_dim(alive_slot_number, active_strip, 1, 1)[:, 0]
        weight = lax.dynamic_slice_in_dim(tapered_precision_factor, active_strip * L, L, 1)
        weights = patch_weights(jnp.take(pert, lists, axis=1), jnp.take(depart, lists, axis=0), weight, counts)
        mesh_verticals = lax.dynamic_slice_in_dim(prior_sample, active_strip * verticals_in_strip, verticals_in_strip, 2)
        npatch = lists.shape[0]
        tile_pieces = mesh_verticals.astype(jnp.float32).reshape(sample_fields, quantity_number, npatch, verticals_in_strip // npatch)
        result = jnp.einsum('jvpc,pjk->kvpc', tile_pieces, weights.astype(jnp.float32))
        return result.reshape(sample_fields, quantity_number, verticals_in_strip).astype(jnp.bfloat16)
    bands = lax.map(one_band, jnp.arange(N_LAT, dtype=jnp.int32))
    return jnp.moveaxis(bands, 0, 2).reshape(sample_fields, quantity_number, vertical_sum_number)
```

```python
import functools
import math

import jax
import jax.numpy as jnp
from jax import lax
from jax.experimental import pallas as pl
from jax.experimental.pallas import tpu as pltpu
from jax.sharding import PartitionSpec as P

MESH = pl.DeviceIdType.MESH
F32, BF16 = jnp.float32, jnp.bfloat16

MEMBERS = 64
MINE = 4
NV = 83
NVP = 88
BAND = 8192
OWN = 512
NG = 4
PATCHES = 32
SLOTS = 512
SPAN = 9
NWT = 48
NOT = 32
NS_STEPS = 8
PAIRS = PATCHES // 2
BATCH = 8
ROWS = (NVP // 8) * (BAND // 128) * 8

ORDER = (
    (1, 0), (0, 2), (3, 0), (2, 1), (0, 1), (2, 3), (0, 3), (1, 2),
    (2, 0), (3, 2), (1, 1), (3, 3), (2, 2), (1, 3), (3, 1),
)


def dot(a, b):
    return jnp.dot(a, b, preferred_element_type=F32)


def dot_t(a, b):
    return lax.dot_general(a, b, (((1,), (1,)), ((), ())), preferred_element_type=F32)


def halves(value):
    high = value.astype(BF16)
    return high, (value - high.astype(F32)).astype(BF16)


def left(value):
    rows = jnp.concatenate(halves(value), axis=0)
    return jnp.concatenate([rows, rows], axis=1)


def right(value, block_mask):
    high, low = halves(value)
    return jnp.concatenate(
        [
            jnp.concatenate([high, high], axis=0) * block_mask,
            jnp.concatenate([low, low], axis=0) * block_mask,
        ],
        axis=0,
    )


def folded(product):
    half = product.shape[0] // 2
    return product[:half] + product[half:]


def kernel(
    prior, spots, columns, tiles, alive, values, lists, taper,
    out,
    mine, table, alone, got, made, equiv32, equiv, every, window, perts, value_win, parts, depart,
    gram, proj, weights, wide, wide_out,
    own_sem, in_send, in_recv, in_own, gather_send, gather_recv, gather_own,
    halo_send, halo_recv, value_send, value_recv, value_own, out_send, out_recv, out_own,
):
    me, lat = lax.axis_index("mem"), lax.axis_index("lat")
    bands = lax.axis_size("lat")
    my_y, my_x = me // 4, me % 4
    partners = [((my_y + dy) % 4) * 4 + (my_x + dx) % 4 for dx, dy in ORDER]
    north, south = (lat + 1) % bands, (lat + bands - 1) % bands

    load = [
        pltpu.make_async_copy(prior.at[j], mine.at[j], own_sem.at[j]) for j in range(MINE)
    ]
    for copy in load:
        copy.start()

    barrier = pltpu.get_barrier_semaphore()
    for partner in partners:
        pl.semaphore_signal(barrier, inc=1, device_id=(partner, lat), device_id_type=MESH)
    for band in (north, south):
        pl.semaphore_signal(barrier, inc=1, device_id=(me, band), device_id_type=MESH)
    pl.semaphore_wait(barrier, len(ORDER) + 2)

    def piece(owner, group):
        return pl.ds(pl.multiple_of(owner * OWN + group * 128, 128), 128)

    my_rows = pl.ds(me * MINE, MINE)

    def copies_in(group):
        sends = [
            pltpu.make_async_remote_copy(
                src_ref=prior.at[:, :, piece(partner, group)],
                dst_ref=got.at[group, my_rows],
                send_sem=in_send.at[group, s],
                recv_sem=in_recv.at[group, s],
                device_id=(partner, lat),
                device_id_type=MESH,
            )
            for s, partner in enumerate(partners)
        ]
        own = pltpu.make_async_copy(
            prior.at[:, :, piece(me, group)], got.at[group, my_rows], in_own.at[group]
        )
        return sends + [own]

    def copies_out(group):
        sends = [
            pltpu.make_async_remote_copy(
                src_ref=made.at[group, pl.ds(partner * MINE, MINE)],
                dst_ref=out.at[:, :, piece(me, group)],
                send_sem=out_send.at[group, s],
                recv_sem=out_recv.at[group, s],
                device_id=(partner, lat),
                device_id_type=MESH,
            )
            for s, partner in enumerate(partners)
        ]
        own = pltpu.make_async_copy(
            made.at[group, my_rows], out.at[:, :, piece(me, group)], out_own.at[group]
        )
        return sends + [own]

    ins = [copies_in(group) for group in range(NG)]
    outs = [copies_out(group) for group in range(NG)]
    for copy in ins[0]:
        copy.start()

    value_copies = [
        pltpu.make_async_remote_copy(
            src_ref=values.at[source],
            dst_ref=value_win.at[target],
            send_sem=value_send.at[k],
            recv_sem=value_recv.at[k],
            device_id=(me, band),
            device_id_type=MESH,
        )
        for k, (source, target, band) in enumerate(((3, 0, north), (0, 5, south)))
    ]
    value_copies.append(pltpu.make_async_copy(values, value_win.at[pl.ds(1, 4)], value_own))
    for copy in value_copies:
        copy.start()

    for copy in load:
        copy.wait()

    def spread_rows(ct, carry):
        lanes = pl.ds(pl.multiple_of(ct * 128, 128), 128)
        for j in range(MINE):
            for v in range(0, NV, 16):
                count = min(16, NV - v)
                block = mine[j, v : v + count, lanes].astype(F32)
                for t in range(0, count, 8):
                    n = min(8, count - t)
                    start = (((v + t) // 8) * (BAND // 128) + ct) * 8 * MINE + j
                    table[pl.ds(start, n, stride=MINE), :] = block[t : t + n]
        return carry

    lax.fori_loop(0, BAND // 128, spread_rows, 0)

    lane4 = lax.broadcasted_iota(jnp.int32, (MINE, 128), 1)
    ones = jnp.ones((8, 128), BF16)

    def pick(ot, carry):
        for i in range(128):
            found = table[pl.ds(spots[ot * 128 + i], MINE), :]
            alone[pl.ds(i, MINE, stride=128), :] = jnp.where(
                lane4 == columns[ot * 128 + i], found, 0.0
            )
        row = dot_t(ones, alone[...].astype(BF16))
        start = (ot // 8) * 8 * MINE + ot % 8
        for j in range(MINE):
            equiv32[pl.ds(start + j * 8, 1), :] = row[0:1, j * 128 : j * 128 + 128]
        return carry

    lax.fori_loop(0, NOT, pick, 0)
    for quarter in range(4):
        equiv[quarter] = equiv32[quarter * 32 : quarter * 32 + 32].astype(BF16)

    gathers = [
        pltpu.make_async_remote_copy(
            src_ref=equiv,
            dst_ref=every.at[pl.ds(1, 4), me],
            send_sem=gather_send.at[s],
            recv_sem=gather_recv.at[s],
            device_id=(partner, lat),
            device_id_type=MESH,
        )
        for s, partner in enumerate(partners)
    ]
    gathers.append(pltpu.make_async_copy(equiv, every.at[pl.ds(1, 4), me], gather_own))
    for copy in gathers:
        copy.start()
    for group in range(1, NG):
        for copy in ins[group]:
            copy.start()
    for copy in gathers:
        copy.wait()
    halos = [
        pltpu.make_async_remote_copy(
            src_ref=every.at[source],
            dst_ref=every.at[target],
            send_sem=halo_send.at[k],
            recv_sem=halo_recv.at[k],
            device_id=(me, band),
            device_id_type=MESH,
        )
        for k, (source, target, band) in enumerate(((4, 0, north), (1, 5, south)))
    ]
    for copy in halos:
        copy.start()

    def spread_members(q, carry):
        for m in range(MEMBERS // MINE):
            block = every[q, m].astype(F32)
            for j in range(MINE):
                start = q * 8 * MEMBERS + m * MINE + j
                window[pl.ds(start, 8, stride=MEMBERS), :] = block[j * 8 : j * 8 + 8]
        return carry

    def center(tile, carry):
        rows = pl.ds(pl.multiple_of(tile * MEMBERS, MEMBERS), MEMBERS)
        field = window[rows, :]
        mean = jnp.sum(field, axis=0, keepdims=True) * (1.0 / MEMBERS)
        pert = field - mean
        perts[tile] = pert
        parts[tile] = jnp.concatenate(halves(pert), axis=0)
        depart[pl.ds(tile, 1), :] = value_win[tile // 8, pl.ds(tile % 8, 1), :] - mean
        return carry

    for copy in value_copies:
        copy.wait()
    lax.fori_loop(1, 5, spread_members, 0)
    lax.fori_loop(8, 40, center, 0)
    for copy in halos:
        copy.wait()
    for quarter in (0, 5):
        spread_members(quarter, 0)
        lax.fori_loop(quarter * 8, quarter * 8 + 8, center, 0)

    slot = lax.broadcasted_iota(jnp.int32, (1, SLOTS), 1)
    high_row = lax.broadcasted_iota(jnp.int32, (16, SLOTS), 0)
    low_row = lax.broadcasted_iota(jnp.int32, (128, SLOTS), 0)
    lane64 = lax.broadcasted_iota(jnp.int32, (MEMBERS, 128), 1)
    row64 = lax.broadcasted_iota(jnp.int32, (MEMBERS, 128), 0)
    first_half = lane64 < MEMBERS
    diagonal = (lane64 % MEMBERS) == row64
    unit = diagonal.astype(F32)
    first_lane = lax.broadcasted_iota(jnp.int32, (1, 128), 1) < MEMBERS

    def one_patch(p):
        base = tiles[p]
        place = lists[pl.ds(p, 1), :] - base * 128
        weight = jnp.where(slot < alive[p], taper[pl.ds(p, 1), :], 0.0)
        hit = high_row == lax.shift_right_arithmetic(place, 7)
        laid = []
        rest = weight
        for _ in range(3):
            part = rest.astype(BF16).astype(F32)
            laid.append(jnp.where(hit, part, 0.0))
            rest = rest - part
        laid = jnp.concatenate(laid, axis=0).astype(BF16)
        lows = jnp.where(low_row == (place & 127), 1.0, 0.0).astype(BF16)
        laid = dot_t(laid, lows)
        laid = laid[0:16] + laid[16:32] + laid[32:48]
        lefts, rights = [], []
        for t in range(SPAN):
            w = laid[t : t + 1]
            tile = base + t
            high, low = halves(perts[tile] * w)
            d_high, d_low = halves(depart[pl.ds(tile, 1), :] * w)
            ends = jnp.concatenate(
                [d_high.astype(F32), d_low.astype(F32), jnp.zeros((14, 128), F32)], axis=0
            )
            lefts.append(jnp.concatenate([high, low, ends.astype(BF16)], axis=0))
            rights.append(parts[tile])
        product = dot_t(jnp.concatenate(lefts, axis=1), jnp.concatenate(rights, axis=1))
        return product

    def fold_first(a, b):
        return a + pltpu.roll(a, MEMBERS, 1) + b

    def fold_second(a, b):
        return a + pltpu.roll(a, MEMBERS, 1) + pltpu.roll(b, MEMBERS, 1)

    def one_pair(k, carry):
        one, two = one_patch(2 * k), one_patch(2 * k + 1)
        both = jnp.where(
            first_half,
            fold_first(one[0:64], one[64:128]),
            fold_second(two[0:64], two[64:128]),
        )
        gram[k] = both + (MEMBERS - 1.0) * unit
        row_one, row_two = one[128:136], two[128:136]
        swapped_one, swapped_two = pltpu.roll(row_one, MEMBERS, 1), pltpu.roll(row_two, MEMBERS, 1)
        end_one = row_one[0:1] + swapped_one[0:1] + row_one[1:2]
        end_two = row_two[0:1] + swapped_two[0:1] + swapped_two[1:2]
        proj[pl.ds(k, 1), :] = jnp.where(first_lane, end_one, end_two)
        return carry

    lax.fori_loop(0, PAIRS, one_pair, 0)

    row128 = lax.broadcasted_iota(jnp.int32, (128, 128), 0)
    lane128 = lax.broadcasted_iota(jnp.int32, (128, 128), 1)
    block_mask = jnp.where((row128 < MEMBERS) == (lane128 < MEMBERS), 1.0, 0.0).astype(BF16)

    def half_sums(value):
        one = jnp.sum(jnp.where(lane64[: value.shape[0]] < MEMBERS, value, 0.0), axis=1, keepdims=True)
        two = jnp.sum(jnp.where(lane64[: value.shape[0]] < MEMBERS, 0.0, value), axis=1, keepdims=True)
        return jnp.where(lane64[: value.shape[0]] < MEMBERS, one, two)

    def batch_of_pairs(batch, carry):
        pairs = [batch * BATCH + i for i in range(BATCH)]
        grams = [gram[k] for k in pairs]
        traces = []
        for g in grams:
            diag = jnp.sum(jnp.where(diagonal, g, 0.0), axis=0, keepdims=True)
            one = jnp.sum(jnp.where(first_lane, diag, 0.0), axis=1, keepdims=True)
            two = jnp.sum(jnp.where(first_lane, 0.0, diag), axis=1, keepdims=True)
            traces.append(jnp.where(first_lane, one, two))
        roots = [g / t for g, t in zip(grams, traces)]
        mids = [1.5 * unit - 0.5 * r for r in roots]
        roots = [folded(dot(left(r), right(m, block_mask))) for r, m in zip(roots, mids)]
        invs = mids

        def sweep(_, state):
            roots, invs = state
            mids = [
                1.5 * unit - 0.5 * folded(dot(left(v), right(r, block_mask)))
                for r, v in zip(roots, invs)
            ]
            new_roots, new_invs = [], []
            for r, v, m in zip(roots, invs, mids):
                both = dot(jnp.concatenate([left(r), left(v)], axis=0), right(m, block_mask))
                new_roots.append(folded(both[0:128]))
                new_invs.append(folded(both[128:256]))
            return new_roots, new_invs

        roots, invs = lax.fori_loop(0, NS_STEPS - 2, sweep, (roots, invs))
        mids = [
            1.5 * unit - 0.5 * folded(dot(left(v), right(r, block_mask)))
            for r, v in zip(roots, invs)
        ]
        invs = [folded(dot(left(v), right(m, block_mask))) for v, m in zip(invs, mids)]

        for k, v, t in zip(pairs, invs, traces):
            factor = right(v, block_mask)
            row = proj[pl.ds(k, 1), :]
            for _ in range(2):
                wide_row = jnp.concatenate([row, jnp.zeros((7, 128), F32)], axis=0)
                row = folded(dot(left(wide_row), factor))[0:1]
            full = v * (math.sqrt(MEMBERS - 1.0) * lax.rsqrt(t)) + row / t
            full = full + (1.0 - half_sums(full)) * (1.0 / MEMBERS)
            weights[k] = full.astype(BF16)
        return carry

    lax.fori_loop(0, PAIRS // BATCH, batch_of_pairs, 0)

    lane_patch = lax.broadcasted_iota(jnp.int32, (16, 128), 1) // 16
    masks = [jnp.where(lane_patch == p, 1.0, 0.0).astype(BF16) for p in range(8)]
    masks = [jnp.concatenate([m] * 4, axis=0) for m in masks]

    for group in range(NG):
        for copy in ins[group]:
            copy.wait()

        def widen(j, carry):
            for v in range(0, NV, 16):
                count = min(16, NV - v)
                wide[pl.ds(j * NVP + v, count), :] = got[group, j, v : v + count].astype(F32)
            return carry

        lax.fori_loop(0, MEMBERS, widen, 0)
        factor = jnp.concatenate([weights[group * 4 + i] for i in range(4)], axis=1)

        def some(first, count):
            fields = []
            for i in range(count):
                field = wide[pl.ds(first + i, MEMBERS, stride=NVP), :].astype(BF16)
                fields.append(jnp.concatenate([field * m for m in masks], axis=0))
            made_here = dot(factor, jnp.concatenate(fields, axis=1))
            for i in range(count):
                wide_out[pl.ds(first + i, MEMBERS, stride=NVP), :] = made_here[:, i * 128 : i * 128 + 128]

        def variables(step, carry):
            some(step * 4, 4)
            return carry

        lax.fori_loop(0, NV // 4, variables, 0)
        some(NV // 4 * 4, NV % 4)

        def narrow(k, carry):
            for v in range(0, NV, 16):
                count = min(16, NV - v)
                made[group, k, v : v + count] = wide_out[pl.ds(k * NVP + v, count), :].astype(BF16)
            return carry

        lax.fori_loop(0, MEMBERS, narrow, 0)
        for copy in outs[group]:
            copy.start()
    for group in range(NG):
        for copy in outs[group]:
            copy.wait()


def on_device(prior, values, quantity, vertical, lists, alive, taper):
    row = ((quantity >> 3) * (BAND // 128) + (vertical >> 7)) * 8 + (quantity & 7)
    spots, columns = row * MINE, vertical & 127
    tiles = jnp.minimum(jnp.min(lists, axis=1) >> 7, NWT - SPAN)
    vmem = pl.BlockSpec(memory_space=pltpu.VMEM)
    smem = pl.BlockSpec(memory_space=pltpu.SMEM)
    dma = pltpu.SemaphoreType.DMA
    peers = len(ORDER)
    return pl.pallas_call(
        kernel,
        out_shape=jax.ShapeDtypeStruct(prior.shape, prior.dtype),
        in_specs=[pl.BlockSpec(memory_space=pl.ANY), smem, smem, smem, smem, vmem, vmem, vmem],
        out_specs=pl.BlockSpec(memory_space=pl.ANY),
        scratch_shapes=[
            pltpu.VMEM((MINE, NV, BAND), BF16),
            pltpu.VMEM((ROWS * MINE, 128), F32),
            pltpu.VMEM((128 * MINE, 128), F32),
            pltpu.VMEM((NG, MEMBERS, NV, 128), BF16),
            pltpu.VMEM((NG, MEMBERS, NV, 128), BF16),
            pltpu.VMEM((NOT * MINE, 128), F32),
            pltpu.VMEM((4, 8 * MINE, 128), BF16),
            pltpu.VMEM((6, MEMBERS // MINE, 8 * MINE, 128), BF16),
            pltpu.VMEM((NWT * MEMBERS, 128), F32),
            pltpu.VMEM((NWT, MEMBERS, 128), F32),
            pltpu.VMEM((6, 8, 128), F32),
            pltpu.VMEM((NWT, 2 * MEMBERS, 128), BF16),
            pltpu.VMEM((NWT, 128), F32),
            pltpu.VMEM((PAIRS, MEMBERS, 128), F32),
            pltpu.VMEM((PAIRS, 128), F32),
            pltpu.VMEM((PAIRS, MEMBERS, 128), BF16),
            pltpu.VMEM((MEMBERS * NVP, 128), F32),
            pltpu.VMEM((MEMBERS * NVP, 128), F32),
            dma((MINE,)),
            dma((NG, peers)), dma((NG, peers)), dma((NG,)),
            dma((peers,)), dma((peers,)), dma,
            dma((2,)), dma((2,)),
            dma((2,)), dma((2,)), dma,
            dma((NG, peers)), dma((NG, peers)), dma((NG,)),
        ],
        compiler_params=pltpu.CompilerParams(
            collective_id=0, has_side_effects=True, vmem_limit_bytes=58 * 2**20
        ),
    )(
        prior,
        spots,
        columns,
        tiles,
        alive[:, 0],
        values.astype(F32).reshape(4, 8, 128),
        lists,
        taper,
    )


def solution(mesh):
    placed = (
        P("mem", None, "lat"),
        P("lat"),
        P("lat"),
        P("lat"),
        P("mem", "lat"),
        P("mem", "lat"),
        P("mem", "lat"),
    )
    return jax.shard_map(
        on_device, mesh=mesh, in_specs=placed, out_specs=P("mem", None, "lat"), check_vma=False
    )
```

```python
import functools
import math

import jax
import jax.numpy as jnp
from jax import lax
from jax.experimental import pallas as pl
from jax.experimental.pallas import tpu as pltpu
from jax.sharding import PartitionSpec as P

MESH = pl.DeviceIdType.MESH
F32, BF16 = jnp.float32, jnp.bfloat16

MEMBERS = 64
MINE = 4
NV = 83
NCT = 64
NG = 4
CHUNKS = ((0, 22), (22, 44), (44, 64), (64, NV))
PATCHES = 32
SLOTS = 512
SPAN = 9
NWT = 48
NOT = 32
NS_STEPS = 8
PAIRS = PATCHES // 2
BATCH = 8

EARLY = 1

ORDER = (
    (1, 0), (0, 2), (3, 0), (2, 1), (0, 1), (2, 3), (0, 3), (1, 2),
    (2, 0), (3, 2), (1, 1), (3, 3), (2, 2), (1, 3), (3, 1),
)


def dot(a, b):
    return jnp.dot(a, b, preferred_element_type=F32)


def dot_t(a, b):
    return lax.dot_general(a, b, (((1,), (1,)), ((), ())), preferred_element_type=F32)


def halves(value):
    high = value.astype(BF16)
    return high, (value - high.astype(F32)).astype(BF16)


def left(value):
    rows = jnp.concatenate(halves(value), axis=0)
    return jnp.concatenate([rows, rows], axis=1)


def right(value, block_mask):
    high, low = halves(value)
    return jnp.concatenate(
        [
            jnp.concatenate([high, high], axis=0) * block_mask,
            jnp.concatenate([low, low], axis=0) * block_mask,
        ],
        axis=0,
    )


def folded(product):
    half = product.shape[0] // 2
    return product[:half] + product[half:]


def kernel(
    prior, quantity, vertical, alive, values, lists, taper,
    out,
    mine, tiles, values32, alone, got, made, equiv32, equiv, every, window, perts, value_win, parts, depart,
    gram, proj, weights, wide, wide_out,
    own_sem, in_send, in_recv, in_own, gather_send, gather_recv, gather_own,
    halo_send, halo_recv, value_send, value_recv, value_own, out_send, out_recv, out_own,
):
    me, lat = lax.axis_index("mem"), lax.axis_index("lat")
    bands = lax.axis_size("lat")
    my_y, my_x = me // 4, me % 4
    partners = [((my_y + dy) % 4) * 4 + (my_x + dx) % 4 for dx, dy in ORDER]
    north, south = (lat + 1) % bands, (lat + bands - 1) % bands

    load = pltpu.make_async_copy(prior, mine, own_sem)
    load.start()

    barrier = pltpu.get_barrier_semaphore()
    for partner in partners:
        pl.semaphore_signal(barrier, inc=1, device_id=(partner, lat), device_id_type=MESH)
    for band in (north, south):
        pl.semaphore_signal(barrier, inc=1, device_id=(me, band), device_id_type=MESH)
    pl.semaphore_wait(barrier, len(ORDER) + 2)

    def piece(owner, chunk):
        return pl.ds(CHUNKS[chunk][0], CHUNKS[chunk][1] - CHUNKS[chunk][0]), pl.ds(owner * NG, NG)

    def block(owner, chunk):
        return pl.ds(CHUNKS[chunk][0], CHUNKS[chunk][1] - CHUNKS[chunk][0]), owner

    def copies_in(chunk):
        sends = [
            pltpu.make_async_remote_copy(
                src_ref=prior.at[piece(partner, chunk)],
                dst_ref=got.at[block(me, chunk)],
                send_sem=in_send.at[chunk, s],
                recv_sem=in_recv.at[chunk, s],
                device_id=(partner, lat),
                device_id_type=MESH,
            )
            for s, partner in enumerate(partners)
        ]
        own = pltpu.make_async_copy(
            prior.at[piece(me, chunk)], got.at[block(me, chunk)], in_own.at[chunk]
        )
        return sends + [own]

    def copies_out(chunk):
        sends = [
            pltpu.make_async_remote_copy(
                src_ref=made.at[block(partner, chunk)],
                dst_ref=out.at[piece(me, chunk)],
                send_sem=out_send.at[chunk, s],
                recv_sem=out_recv.at[chunk, s],
                device_id=(partner, lat),
                device_id_type=MESH,
            )
            for s, partner in enumerate(partners)
        ]
        own = pltpu.make_async_copy(
            made.at[block(me, chunk)], out.at[piece(me, chunk)], out_own.at[chunk]
        )
        return sends + [own]

    ins = [copies_in(chunk) for chunk in range(len(CHUNKS))]
    outs = [copies_out(chunk) for chunk in range(len(CHUNKS))]
    for copy in ins[0]:
        copy.start()

    values32[...] = values[...].astype(F32)
    value_copies = [
        pltpu.make_async_remote_copy(
            src_ref=values32.at[source],
            dst_ref=value_win.at[target],
            send_sem=value_send.at[k],
            recv_sem=value_recv.at[k],
            device_id=(me, band),
            device_id_type=MESH,
        )
        for k, (source, target, band) in enumerate(((3, 0, north), (0, 5, south)))
    ]
    value_copies.append(pltpu.make_async_copy(values32, value_win.at[pl.ds(1, 4)], value_own))
    for copy in value_copies:
        copy.start()

    def first_tile(p, carry):
        tiles[p] = jnp.minimum(lax.shift_right_logical(jnp.min(lists[pl.ds(p, 1), :]), 7), NWT - SPAN)
        return carry

    lax.fori_loop(0, PATCHES, first_tile, 0)

    lane4 = lax.broadcasted_iota(jnp.int32, (MINE, 128), 1)
    ones = jnp.ones((8, 128), BF16)

    load.wait()

    def pick(ot, carry):
        for i in range(128):
            column = vertical[ot * 128 + i]
            found = mine[quantity[ot * 128 + i], lax.shift_right_logical(column, 7)].astype(F32)
            alone[pl.ds(i, MINE, stride=128), :] = jnp.where(lane4 == (column & 127), found, 0.0)
        row = dot_t(ones, alone[...].astype(BF16))
        start = (ot // 8) * 8 * MINE + ot % 8
        for j in range(MINE):
            equiv32[pl.ds(start + j * 8, 1), :] = row[0:1, j * 128 : j * 128 + 128]
        return carry

    lax.fori_loop(0, NOT, pick, 0)
    for quarter in range(4):
        equiv[quarter] = equiv32[quarter * 32 : quarter * 32 + 32].astype(BF16)

    side_x = [my_y * 4 + (my_x + d) % 4 for d in (1, 3, 2)]
    side_y = [((my_y + d) % 4) * 4 + my_x for d in (1, 3, 2)]
    first, second = pl.ds(1, 2), pl.ds(3, 2)

    def gather(source, target, k, partner):
        return pltpu.make_async_remote_copy(
            src_ref=source,
            dst_ref=target,
            send_sem=gather_send.at[k],
            recv_sem=gather_recv.at[k],
            device_id=(partner, lat),
            device_id_type=MESH,
        )

    gathers = [
        gather(equiv.at[pl.ds(0, 2)], every.at[first, my_y, my_x], k, partner)
        for k, partner in enumerate(side_x)
    ]
    gathers += [
        gather(equiv.at[pl.ds(2, 2)], every.at[second, my_y, my_x], 3 + k, partner)
        for k, partner in enumerate(side_y)
    ]
    gathers.append(pltpu.make_async_copy(equiv, every.at[pl.ds(1, 4), my_y, my_x], gather_own))
    for copy in gathers:
        copy.start()
    for chunk in range(1, EARLY):
        for copy in ins[chunk]:
            copy.start()
    for copy in gathers:
        copy.wait()
    gathers = [
        gather(every.at[first, my_y], every.at[first, my_y], 6 + k, partner)
        for k, partner in enumerate(side_y)
    ]
    gathers += [
        gather(every.at[second, :, my_x], every.at[second, :, my_x], 9 + k, partner)
        for k, partner in enumerate(side_x)
    ]
    for copy in gathers:
        copy.start()
    for chunk in range(EARLY, len(CHUNKS)):
        for copy in ins[chunk]:
            copy.start()
    for copy in gathers:
        copy.wait()
    halos = [
        pltpu.make_async_remote_copy(
            src_ref=every.at[source],
            dst_ref=every.at[target],
            send_sem=halo_send.at[k],
            recv_sem=halo_recv.at[k],
            device_id=(me, band),
            device_id_type=MESH,
        )
        for k, (source, target, band) in enumerate(((4, 0, north), (1, 5, south)))
    ]
    for copy in halos:
        copy.start()

    def spread_members(q, carry):
        for m in range(MEMBERS // MINE):
            block = every[q, m // 4, m % 4].astype(F32)
            for j in range(MINE):
                start = q * 8 * MEMBERS + m * MINE + j
                window[pl.ds(start, 8, stride=MEMBERS), :] = block[j * 8 : j * 8 + 8]
        return carry

    def center(tile, carry):
        rows = pl.ds(pl.multiple_of(tile * MEMBERS, MEMBERS), MEMBERS)
        field = window[rows, :]
        mean = jnp.sum(field, axis=0, keepdims=True) * (1.0 / MEMBERS)
        pert = field - mean
        perts[tile] = pert
        parts[tile] = jnp.concatenate(halves(pert), axis=0)
        depart[pl.ds(tile, 1), :] = value_win[tile // 8, pl.ds(tile % 8, 1), :] - mean
        return carry

    for copy in value_copies:
        copy.wait()
    lax.fori_loop(1, 5, spread_members, 0)
    lax.fori_loop(8, 40, center, 0)
    for copy in halos:
        copy.wait()
    for quarter in (0, 5):
        spread_members(quarter, 0)
        lax.fori_loop(quarter * 8, quarter * 8 + 8, center, 0)

    slot = lax.broadcasted_iota(jnp.int32, (1, SLOTS), 1)
    high_row = lax.broadcasted_iota(jnp.int32, (16, SLOTS), 0)
    low_row = lax.broadcasted_iota(jnp.int32, (128, SLOTS), 0)
    lane64 = lax.broadcasted_iota(jnp.int32, (MEMBERS, 128), 1)
    row64 = lax.broadcasted_iota(jnp.int32, (MEMBERS, 128), 0)
    first_half = lane64 < MEMBERS
    diagonal = (lane64 % MEMBERS) == row64
    unit = diagonal.astype(F32)
    first_lane = lax.broadcasted_iota(jnp.int32, (1, 128), 1) < MEMBERS

    def one_patch(p):
        base = tiles[p]
        place = lists[pl.ds(p, 1), :] - base * 128
        weight = jnp.where(slot < alive[p], taper[pl.ds(p, 1), :], 0.0)
        hit = high_row == lax.shift_right_arithmetic(place, 7)
        laid = []
        rest = weight
        for _ in range(3):
            part = rest.astype(BF16).astype(F32)
            laid.append(jnp.where(hit, part, 0.0))
            rest = rest - part
        laid = jnp.concatenate(laid, axis=0).astype(BF16)
        lows = jnp.where(low_row == (place & 127), 1.0, 0.0).astype(BF16)
        laid = dot_t(laid, lows)
        laid = laid[0:16] + laid[16:32] + laid[32:48]
        lefts, rights = [], []
        for t in range(SPAN):
            w = laid[t : t + 1]
            tile = base + t
            high, low = halves(perts[tile] * w)
            d_high, d_low = halves(depart[pl.ds(tile, 1), :] * w)
            ends = jnp.concatenate(
                [d_high.astype(F32), d_low.astype(F32), jnp.zeros((14, 128), F32)], axis=0
            )
            lefts.append(jnp.concatenate([high, low, ends.astype(BF16)], axis=0))
            rights.append(parts[tile])
        product = dot_t(jnp.concatenate(lefts, axis=1), jnp.concatenate(rights, axis=1))
        return product

    def fold_first(a, b):
        return a + pltpu.roll(a, MEMBERS, 1) + b

    def fold_second(a, b):
        return a + pltpu.roll(a, MEMBERS, 1) + pltpu.roll(b, MEMBERS, 1)

    def one_pair(k, carry):
        one, two = one_patch(2 * k), one_patch(2 * k + 1)
        both = jnp.where(
            first_half,
            fold_first(one[0:64], one[64:128]),
            fold_second(two[0:64], two[64:128]),
        )
        gram[k] = both + (MEMBERS - 1.0) * unit
        row_one, row_two = one[128:136], two[128:136]
        swapped_one, swapped_two = pltpu.roll(row_one, MEMBERS, 1), pltpu.roll(row_two, MEMBERS, 1)
        end_one = row_one[0:1] + swapped_one[0:1] + row_one[1:2]
        end_two = row_two[0:1] + swapped_two[0:1] + swapped_two[1:2]
        proj[pl.ds(k, 1), :] = jnp.where(first_lane, end_one, end_two)
        return carry

    lax.fori_loop(0, PAIRS, one_pair, 0)

    row128 = lax.broadcasted_iota(jnp.int32, (128, 128), 0)
    lane128 = lax.broadcasted_iota(jnp.int32, (128, 128), 1)
    block_mask = jnp.where((row128 < MEMBERS) == (lane128 < MEMBERS), 1.0, 0.0).astype(BF16)

    def half_sums(value):
        one = jnp.sum(jnp.where(lane64[: value.shape[0]] < MEMBERS, value, 0.0), axis=1, keepdims=True)
        two = jnp.sum(jnp.where(lane64[: value.shape[0]] < MEMBERS, 0.0, value), axis=1, keepdims=True)
        return jnp.where(lane64[: value.shape[0]] < MEMBERS, one, two)

    def batch_of_pairs(batch, carry):
        pairs = [batch * BATCH + i for i in range(BATCH)]
        grams = [gram[k] for k in pairs]
        traces = []
        for g in grams:
            diag = jnp.sum(jnp.where(diagonal, g, 0.0), axis=0, keepdims=True)
            one = jnp.sum(jnp.where(first_lane, diag, 0.0), axis=1, keepdims=True)
            two = jnp.sum(jnp.where(first_lane, 0.0, diag), axis=1, keepdims=True)
            traces.append(jnp.where(first_lane, one, two))
        roots = [g / t for g, t in zip(grams, traces)]
        mids = [1.5 * unit - 0.5 * r for r in roots]
        roots = [folded(dot(left(r), right(m, block_mask))) for r, m in zip(roots, mids)]
        invs = mids

        def sweep(_, state):
            roots, invs = state
            mids = [
                1.5 * unit - 0.5 * folded(dot(left(v), right(r, block_mask)))
                for r, v in zip(roots, invs)
            ]
            new_roots, new_invs = [], []
            for r, v, m in zip(roots, invs, mids):
                both = dot(jnp.concatenate([left(r), left(v)], axis=0), right(m, block_mask))
                new_roots.append(folded(both[0:128]))
                new_invs.append(folded(both[128:256]))
            return new_roots, new_invs

        roots, invs = lax.fori_loop(0, NS_STEPS - 2, sweep, (roots, invs))
        mids = [
            1.5 * unit - 0.5 * folded(dot(left(v), right(r, block_mask)))
            for r, v in zip(roots, invs)
        ]
        invs = [folded(dot(left(v), right(m, block_mask))) for v, m in zip(invs, mids)]

        for k, v, t in zip(pairs, invs, traces):
            factor = right(v, block_mask)
            row = proj[pl.ds(k, 1), :]
            for _ in range(2):
                wide_row = jnp.concatenate([row, jnp.zeros((7, 128), F32)], axis=0)
                row = folded(dot(left(wide_row), factor))[0:1]
            full = v * (math.sqrt(MEMBERS - 1.0) * lax.rsqrt(t)) + row / t
            full = full + (1.0 - half_sums(full)) * (1.0 / MEMBERS)
            weights[k] = full.astype(BF16)
        return carry

    lax.fori_loop(0, PAIRS // BATCH, batch_of_pairs, 0)

    lane_patch = lax.broadcasted_iota(jnp.int32, (MEMBERS, 128), 1) // 16
    masks = [jnp.where(lane_patch == p, 1.0, 0.0).astype(BF16) for p in range(8)]
    factors = [
        jnp.concatenate([weights[group * 4 + i] for i in range(4)], axis=1) for group in range(NG)
    ]

    def some(first, count):
        for group in range(NG):
            for i in range(count):
                for m in range(MEMBERS // MINE):
                    wide[group, i, m * MINE : m * MINE + MINE] = got[first + i, m, group].astype(F32)
        for group in range(NG):
            fields = []
            for i in range(count):
                field = wide[group, i].astype(BF16)
                fields.append(jnp.concatenate([field * m for m in masks], axis=0))
            result = dot(factors[group], jnp.concatenate(fields, axis=1))
            for i in range(count):
                wide_out[group, i] = result[:, i * 128 : i * 128 + 128]
        for group in range(NG):
            for i in range(count):
                for m in range(MEMBERS // MINE):
                    made[first + i, m, group] = wide_out[
                        group, i, m * MINE : m * MINE + MINE
                    ].astype(BF16)

    for chunk, (start, stop) in enumerate(CHUNKS):
        for copy in ins[chunk]:
            copy.wait()

        def variables(step, carry, start=start):
            some(start + step * 2, 2)
            return carry

        lax.fori_loop(0, (stop - start) // 2, variables, 0)
        if (stop - start) % 2:
            some(stop - 1, 1)
        for copy in outs[chunk]:
            copy.start()
    for chunk in range(len(CHUNKS)):
        for copy in outs[chunk]:
            copy.wait()


def keeper(made, out, held, reads, writes):
    parts = [pl.ds(start, stop - start) for start, stop in CHUNKS]
    copies_in = [
        pltpu.make_async_copy(made.at[part], held.at[part], reads.at[k])
        for k, part in enumerate(parts)
    ]
    copies_out = [
        pltpu.make_async_copy(held.at[part], out.at[part], writes.at[k])
        for k, part in enumerate(parts)
    ]
    for copy in copies_in:
        copy.start()
    for read, write in zip(copies_in, copies_out):
        read.wait()
        write.start()
    for copy in copies_out:
        copy.wait()


def on_device(prior, values, quantity, vertical, lists, alive, taper):
    vmem = pl.BlockSpec(memory_space=pltpu.VMEM)
    smem = pl.BlockSpec(memory_space=pltpu.SMEM)
    dma = pltpu.SemaphoreType.DMA
    peers, chunks = len(ORDER), len(CHUNKS)
    shape = (NV, NCT, MINE, 128)
    prior = prior.reshape(MINE, NV, NCT, 128).transpose(1, 2, 0, 3)
    result = pl.pallas_call(
        kernel,
        out_shape=jax.ShapeDtypeStruct(shape, prior.dtype),
        in_specs=[pl.BlockSpec(memory_space=pl.ANY), smem, smem, smem, vmem, vmem, vmem],
        out_specs=pl.BlockSpec(memory_space=pl.ANY),
        scratch_shapes=[
            pltpu.VMEM((NV, NCT, MINE, 128), BF16),
            pltpu.SMEM((PATCHES,), jnp.int32),
            pltpu.VMEM((4, 8, 128), F32),
            pltpu.VMEM((128 * MINE, 128), F32),
            pltpu.VMEM((NV, MEMBERS // MINE, NG, MINE, 128), BF16),
            pltpu.VMEM((NV, MEMBERS // MINE, NG, MINE, 128), BF16),
            pltpu.VMEM((NOT * MINE, 128), F32),
            pltpu.VMEM((4, 8 * MINE, 128), BF16),
            pltpu.VMEM((6, 4, 4, 8 * MINE, 128), BF16),
            pltpu.VMEM((NWT * MEMBERS, 128), F32),
            pltpu.VMEM((NWT, MEMBERS, 128), F32),
            pltpu.VMEM((6, 8, 128), F32),
            pltpu.VMEM((NWT, 2 * MEMBERS, 128), BF16),
            pltpu.VMEM((NWT, 128), F32),
            pltpu.VMEM((PAIRS, MEMBERS, 128), F32),
            pltpu.VMEM((PAIRS, 128), F32),
            pltpu.VMEM((PAIRS, MEMBERS, 128), BF16),
            pltpu.VMEM((NG, 2, MEMBERS, 128), F32),
            pltpu.VMEM((NG, 2, MEMBERS, 128), F32),
            dma,
            dma((chunks, peers)), dma((chunks, peers)), dma((chunks,)),
            dma((12,)), dma((12,)), dma,
            dma((2,)), dma((2,)),
            dma((2,)), dma((2,)), dma,
            dma((chunks, peers)), dma((chunks, peers)), dma((chunks,)),
        ],
        compiler_params=pltpu.CompilerParams(
            collective_id=0, has_side_effects=True, vmem_limit_bytes=58 * 2**20
        ),
    )(
        prior,
        quantity,
        vertical,
        alive[:, 0],
        values.reshape(4, 8, 128),
        lists,
        taper,
    )
    result = pl.pallas_call(
        keeper,
        out_shape=jax.ShapeDtypeStruct(shape, prior.dtype),
        in_specs=[pl.BlockSpec(memory_space=pl.ANY)],
        out_specs=pl.BlockSpec(memory_space=pl.ANY),
        scratch_shapes=[pltpu.VMEM(shape, BF16), dma((chunks,)), dma((chunks,))],
        compiler_params=pltpu.CompilerParams(vmem_limit_bytes=58 * 2**20),
    )(result)
    return result.transpose(2, 0, 1, 3).reshape(MINE, NV, NCT * 128)


def solution(mesh):
    placed = (
        P("mem", None, "lat"),
        P("lat"),
        P("lat"),
        P("lat"),
        P("mem", "lat"),
        P("mem", "lat"),
        P("mem", "lat"),
    )
    return jax.shard_map(
        on_device, mesh=mesh, in_specs=placed, out_specs=P("mem", None, "lat"), check_vma=False
    )
```

```python
import functools
import math

import jax
import jax.numpy as jnp
from jax import lax
from jax.experimental import pallas as pl
from jax.experimental.pallas import tpu as pltpu
from jax.sharding import PartitionSpec as P

MESH = pl.DeviceIdType.MESH
F32, BF16 = jnp.float32, jnp.bfloat16

MEMBERS = 64
MINE = 4
NV = 83
NCT = 64
BAND = NCT * 128
NG = 4
CHUNKS = tuple((NV * i // 8, NV * (i + 1) // 8) for i in range(8))
PATCHES = 32
SLOTS = 512
SPAN = 9
NWT = 48
NOT = 32
NS_STEPS = 8
PAIRS = PATCHES // 2
BATCH = 16

KEEP = 4
FIRST = 2
EARLY = 3

ORDER = (
    (2, 2), (2, 3), (3, 2), (1, 2), (2, 1), (3, 3), (1, 3), (0, 2),
    (3, 1), (1, 1), (2, 0), (0, 3), (0, 1), (3, 0), (1, 0),
)


def dot(a, b):
    return jnp.dot(a, b, preferred_element_type=F32)


def dot_t(a, b):
    return lax.dot_general(a, b, (((1,), (1,)), ((), ())), preferred_element_type=F32)


def halves(value):
    high = value.astype(BF16)
    return high, (value - high.astype(F32)).astype(BF16)


def left(value):
    rows = jnp.concatenate(halves(value), axis=0)
    return jnp.concatenate([rows, rows], axis=1)


def right(value, block_mask):
    high, low = halves(value)
    return jnp.concatenate(
        [
            jnp.concatenate([high, high], axis=0) * block_mask,
            jnp.concatenate([low, low], axis=0) * block_mask,
        ],
        axis=0,
    )


def folded(product):
    half = product.shape[0] // 2
    return product[:half] + product[half:]


def kernel(
    prior, flat, codes, alive, values, lists, taper,
    out,
    mine, tiles, values32, alone, got, made, equiv32, equiv, every, window, perts, value_win, parts, depart,
    gram, proj, weights, wide, wide_out,
    own_sem, in_send, in_recv, in_own, gather_send, gather_recv, gather_own,
    halo_send, halo_recv, value_send, value_recv, value_own, out_send, out_recv, out_own,
):
    me, lat = lax.axis_index("mem"), lax.axis_index("lat")
    bands = lax.axis_size("lat")
    my_y, my_x = me // 4, me % 4
    turn = 1 - 2 * (lat % 2)
    partners = [
        ((my_y + turn * dy + 4) % 4) * 4 + (my_x + turn * dx + 4) % 4 for dx, dy in ORDER
    ]
    north, south = (lat + 1) % bands, (lat + bands - 1) % bands

    load = pltpu.make_async_copy(flat, mine, own_sem)
    load.start()

    barrier = pltpu.get_barrier_semaphore()
    for partner in partners:
        pl.semaphore_signal(barrier, inc=1, device_id=(partner, lat), device_id_type=MESH)
    for band in (north, south):
        pl.semaphore_signal(barrier, inc=1, device_id=(me, band), device_id_type=MESH)
    pl.semaphore_wait(barrier, len(ORDER) + 2)

    def piece(owner, chunk):
        return pl.ds(CHUNKS[chunk][0], CHUNKS[chunk][1] - CHUNKS[chunk][0]), pl.ds(owner * NG, NG)

    def block(owner, chunk):
        return pl.ds(CHUNKS[chunk][0], CHUNKS[chunk][1] - CHUNKS[chunk][0]), owner

    def copies_in(chunk):
        sends = [
            pltpu.make_async_remote_copy(
                src_ref=prior.at[piece(partner, chunk)],
                dst_ref=got.at[block(me, chunk)],
                send_sem=in_send.at[chunk, s],
                recv_sem=in_recv.at[chunk, s],
                device_id=(partner, lat),
                device_id_type=MESH,
            )
            for s, partner in enumerate(partners)
        ]
        own = pltpu.make_async_copy(
            prior.at[piece(me, chunk)], got.at[block(me, chunk)], in_own.at[chunk]
        )
        return sends + [own]

    def copies_out(chunk):
        sends = [
            pltpu.make_async_remote_copy(
                src_ref=made.at[block(partner, chunk)],
                dst_ref=out.at[piece(me, chunk)],
                send_sem=out_send.at[chunk, s],
                recv_sem=out_recv.at[chunk, s],
                device_id=(partner, lat),
                device_id_type=MESH,
            )
            for s, partner in enumerate(partners)
        ]
        own = pltpu.make_async_copy(
            made.at[block(me, chunk)], out.at[piece(me, chunk)], out_own.at[chunk]
        )
        return sends + [own]

    ins = [copies_in(chunk) for chunk in range(len(CHUNKS))]
    outs = [copies_out(chunk) for chunk in range(len(CHUNKS))]
    for chunk in range(FIRST):
        for copy in ins[chunk]:
            copy.start()

    values32[...] = values[...].astype(F32)
    value_copies = [
        pltpu.make_async_remote_copy(
            src_ref=values32.at[source],
            dst_ref=value_win.at[target],
            send_sem=value_send.at[k],
            recv_sem=value_recv.at[k],
            device_id=(me, band),
            device_id_type=MESH,
        )
        for k, (source, target, band) in enumerate(((3, 0, north), (0, 5, south)))
    ]
    value_copies.append(pltpu.make_async_copy(values32, value_win.at[pl.ds(1, 4)], value_own))
    for copy in value_copies:
        copy.start()

    lane4 = lax.broadcasted_iota(jnp.int32, (MINE, 128), 1)
    ones = jnp.ones((8, 128), BF16)

    load.wait()

    def pick(ot, carry):
        for i in range(128):
            code = codes[ot * 128 + i]
            found = mine[lax.shift_right_logical(code, 7)].astype(F32)
            alone[i * MINE : i * MINE + MINE] = jnp.where(lane4 == (code & 127), found, 0.0)
        sorted_rows = [alone[pl.ds(j, 128, stride=MINE), :].astype(BF16) for j in range(MINE)]
        row = dot_t(ones, jnp.concatenate(sorted_rows, axis=0))
        start = (ot // 8) * 8 * MINE + ot % 8
        for j in range(MINE):
            equiv32[pl.ds(start + j * 8, 1), :] = row[0:1, j * 128 : j * 128 + 128]
        return carry

    lax.fori_loop(0, NOT, pick, 0)
    for quarter in range(4):
        equiv[quarter] = equiv32[quarter * 32 : quarter * 32 + 32].astype(BF16)

    side_x = [my_y * 4 + (my_x + d) % 4 for d in (1, 3, 2)]
    side_y = [((my_y + d) % 4) * 4 + my_x for d in (1, 3, 2)]
    first, second = pl.ds(1, 2), pl.ds(3, 2)

    def gather(source, target, k, partner):
        return pltpu.make_async_remote_copy(
            src_ref=source,
            dst_ref=target,
            send_sem=gather_send.at[k],
            recv_sem=gather_recv.at[k],
            device_id=(partner, lat),
            device_id_type=MESH,
        )

    gathers = [
        gather(equiv.at[pl.ds(0, 2)], every.at[first, my_y, my_x], k, partner)
        for k, partner in enumerate(side_x)
    ]
    gathers += [
        gather(equiv.at[pl.ds(2, 2)], every.at[second, my_y, my_x], 3 + k, partner)
        for k, partner in enumerate(side_y)
    ]
    gathers.append(pltpu.make_async_copy(equiv, every.at[pl.ds(1, 4), my_y, my_x], gather_own))
    for copy in gathers:
        copy.start()
    for chunk in range(FIRST, EARLY):
        for copy in ins[chunk]:
            copy.start()
    def first_tile(p, carry):
        tiles[p] = jnp.minimum(lax.shift_right_logical(jnp.min(lists[pl.ds(p, 1), :]), 7), NWT - SPAN)
        return carry

    lax.fori_loop(0, PATCHES, first_tile, 0)

    for copy in gathers:
        copy.wait()
    gathers = [
        gather(every.at[first, my_y], every.at[first, my_y], 6 + k, partner)
        for k, partner in enumerate(side_y)
    ]
    gathers += [
        gather(every.at[second, :, my_x], every.at[second, :, my_x], 9 + k, partner)
        for k, partner in enumerate(side_x)
    ]
    for copy in gathers:
        copy.start()
    for chunk in range(EARLY, len(CHUNKS)):
        for copy in ins[chunk]:
            copy.start()
    for copy in gathers:
        copy.wait()
    halos = [
        pltpu.make_async_remote_copy(
            src_ref=every.at[source],
            dst_ref=every.at[target],
            send_sem=halo_send.at[k],
            recv_sem=halo_recv.at[k],
            device_id=(me, band),
            device_id_type=MESH,
        )
        for k, (source, target, band) in enumerate(((4, 0, north), (1, 5, south)))
    ]
    for copy in halos:
        copy.start()

    def spread_members(q, carry):
        for m in range(MEMBERS // MINE):
            block = every[q, m // 4, m % 4].astype(F32)
            for j in range(MINE):
                start = q * 8 * MEMBERS + m * MINE + j
                window[pl.ds(start, 8, stride=MEMBERS), :] = block[j * 8 : j * 8 + 8]
        return carry

    def center(tile, carry):
        rows = pl.ds(pl.multiple_of(tile * MEMBERS, MEMBERS), MEMBERS)
        field = window[rows, :]
        mean = jnp.sum(field, axis=0, keepdims=True) * (1.0 / MEMBERS)
        pert = field - mean
        perts[tile] = pert
        parts[tile] = jnp.concatenate(halves(pert), axis=0)
        depart[pl.ds(tile, 1), :] = value_win[tile // 8, pl.ds(tile % 8, 1), :] - mean
        return carry

    for copy in value_copies:
        copy.wait()
    lax.fori_loop(1, 5, spread_members, 0)
    lax.fori_loop(8, 40, center, 0)
    for copy in halos:
        copy.wait()
    for quarter in (0, 5):
        spread_members(quarter, 0)
        lax.fori_loop(quarter * 8, quarter * 8 + 8, center, 0)

    slot = lax.broadcasted_iota(jnp.int32, (1, SLOTS), 1)
    high_row = lax.broadcasted_iota(jnp.int32, (16, SLOTS), 0)
    low_row = lax.broadcasted_iota(jnp.int32, (128, SLOTS), 0)
    lane64 = lax.broadcasted_iota(jnp.int32, (MEMBERS, 128), 1)
    row64 = lax.broadcasted_iota(jnp.int32, (MEMBERS, 128), 0)
    first_half = lane64 < MEMBERS
    diagonal = (lane64 % MEMBERS) == row64
    unit = diagonal.astype(F32)
    first_lane = lax.broadcasted_iota(jnp.int32, (1, 128), 1) < MEMBERS

    def one_patch(p):
        base = tiles[p]
        place = lists[pl.ds(p, 1), :] - base * 128
        weight = jnp.where(slot < alive[p], taper[pl.ds(p, 1), :], 0.0)
        hit = high_row == lax.shift_right_arithmetic(place, 7)
        laid = []
        rest = weight
        for _ in range(3):
            part = rest.astype(BF16).astype(F32)
            laid.append(jnp.where(hit, part, 0.0))
            rest = rest - part
        laid = jnp.concatenate(laid, axis=0).astype(BF16)
        lows = jnp.where(low_row == (place & 127), 1.0, 0.0).astype(BF16)
        laid = dot_t(laid, lows)
        laid = laid[0:16] + laid[16:32] + laid[32:48]
        lefts, rights = [], []
        for t in range(SPAN):
            w = laid[t : t + 1]
            tile = base + t
            high, low = halves(perts[tile] * w)
            d_high, d_low = halves(depart[pl.ds(tile, 1), :] * w)
            ends = jnp.concatenate(
                [d_high.astype(F32), d_low.astype(F32), jnp.zeros((14, 128), F32)], axis=0
            )
            lefts.append(jnp.concatenate([high, low, ends.astype(BF16)], axis=0))
            rights.append(parts[tile])
        product = dot_t(jnp.concatenate(lefts, axis=1), jnp.concatenate(rights, axis=1))
        return product

    def fold_first(a, b):
        return a + pltpu.roll(a, MEMBERS, 1) + b

    def fold_second(a, b):
        return a + pltpu.roll(a, MEMBERS, 1) + pltpu.roll(b, MEMBERS, 1)

    def one_pair(k, carry):
        one, two = one_patch(2 * k), one_patch(2 * k + 1)
        both = jnp.where(
            first_half,
            fold_first(one[0:64], one[64:128]),
            fold_second(two[0:64], two[64:128]),
        )
        gram[k] = both + (MEMBERS - 1.0) * unit
        row_one, row_two = one[128:136], two[128:136]
        swapped_one, swapped_two = pltpu.roll(row_one, MEMBERS, 1), pltpu.roll(row_two, MEMBERS, 1)
        end_one = row_one[0:1] + swapped_one[0:1] + row_one[1:2]
        end_two = row_two[0:1] + swapped_two[0:1] + swapped_two[1:2]
        proj[pl.ds(k, 1), :] = jnp.where(first_lane, end_one, end_two)
        return carry

    lax.fori_loop(0, PAIRS, one_pair, 0)

    row128 = lax.broadcasted_iota(jnp.int32, (128, 128), 0)
    lane128 = lax.broadcasted_iota(jnp.int32, (128, 128), 1)
    block_mask = jnp.where((row128 < MEMBERS) == (lane128 < MEMBERS), 1.0, 0.0).astype(BF16)

    def half_sums(value):
        one = jnp.sum(jnp.where(lane64[: value.shape[0]] < MEMBERS, value, 0.0), axis=1, keepdims=True)
        two = jnp.sum(jnp.where(lane64[: value.shape[0]] < MEMBERS, 0.0, value), axis=1, keepdims=True)
        return jnp.where(lane64[: value.shape[0]] < MEMBERS, one, two)

    def batch_of_pairs(batch, carry):
        pairs = [batch * BATCH + i for i in range(BATCH)]
        grams = [gram[k] for k in pairs]
        traces = []
        for g in grams:
            diag = jnp.sum(jnp.where(diagonal, g, 0.0), axis=0, keepdims=True)
            one = jnp.sum(jnp.where(first_lane, diag, 0.0), axis=1, keepdims=True)
            two = jnp.sum(jnp.where(first_lane, 0.0, diag), axis=1, keepdims=True)
            traces.append(jnp.where(first_lane, one, two))
        roots = [g / t for g, t in zip(grams, traces)]
        mids = [1.5 * unit - 0.5 * r for r in roots]
        roots = [folded(dot(left(r), right(m, block_mask))) for r, m in zip(roots, mids)]
        invs = mids

        def sweep(_, state):
            roots, invs = state
            mids = [
                1.5 * unit - 0.5 * folded(dot(left(v), right(r, block_mask)))
                for r, v in zip(roots, invs)
            ]
            new_roots, new_invs = [], []
            for r, v, m in zip(roots, invs, mids):
                both = dot(jnp.concatenate([left(r), left(v)], axis=0), right(m, block_mask))
                new_roots.append(folded(both[0:128]))
                new_invs.append(folded(both[128:256]))
            return new_roots, new_invs

        roots, invs = lax.fori_loop(0, NS_STEPS - 2, sweep, (roots, invs))
        mids = [
            1.5 * unit - 0.5 * folded(dot(left(v), right(r, block_mask)))
            for r, v in zip(roots, invs)
        ]
        invs = [folded(dot(left(v), right(m, block_mask))) for v, m in zip(invs, mids)]

        for k, v, t in zip(pairs, invs, traces):
            factor = right(v, block_mask)
            row = proj[pl.ds(k, 1), :]
            for _ in range(2):
                wide_row = jnp.concatenate([row, jnp.zeros((7, 128), F32)], axis=0)
                row = folded(dot(left(wide_row), factor))[0:1]
            full = v * (math.sqrt(MEMBERS - 1.0) * lax.rsqrt(t)) + row / t
            full = full + (1.0 - half_sums(full)) * (1.0 / MEMBERS)
            weights[k] = full.astype(BF16)
        return carry

    lax.fori_loop(0, PAIRS // BATCH, batch_of_pairs, 0)

    lane_patch = lax.broadcasted_iota(jnp.int32, (MEMBERS, 128), 1) // 16
    masks = [jnp.where(lane_patch == p, 1.0, 0.0).astype(BF16) for p in range(8)]
    factors = [
        jnp.concatenate([weights[group * 4 + i] for i in range(4)], axis=1) for group in range(NG)
    ]

    def some(first, count):
        for group in range(NG):
            for i in range(count):
                for m in range(MEMBERS // MINE):
                    wide[group, i, m * MINE : m * MINE + MINE] = got[first + i, m, group].astype(F32)
        for group in range(NG):
            fields = []
            for i in range(count):
                field = wide[group, i].astype(BF16)
                fields.append(jnp.concatenate([field * m for m in masks], axis=0))
            result = dot(factors[group], jnp.concatenate(fields, axis=1))
            for i in range(count):
                wide_out[group, i] = result[:, i * 128 : i * 128 + 128]
        for group in range(NG):
            for i in range(count):
                for m in range(MEMBERS // MINE):
                    made[first + i, m, group] = wide_out[
                        group, i, m * MINE : m * MINE + MINE
                    ].astype(BF16)

    for chunk, (start, stop) in enumerate(CHUNKS):
        for copy in ins[chunk]:
            copy.wait()

        def variables(step, carry, start=start):
            some(start + step * 2, 2)
            return carry

        lax.fori_loop(0, (stop - start) // 2, variables, 0)
        if (stop - start) % 2:
            some(stop - 1, 1)
        for copy in outs[chunk]:
            copy.start()
    for chunk in range(len(CHUNKS)):
        for copy in outs[chunk]:
            copy.wait()


def keeper(made, out, writes):
    bounds = [NV * i // KEEP for i in range(KEEP + 1)]
    copies = [
        pltpu.make_async_copy(
            made.at[pl.ds(start, stop - start)], out.at[pl.ds(start, stop - start)], writes.at[k]
        )
        for k, (start, stop) in enumerate(zip(bounds, bounds[1:]))
    ]
    for copy in copies:
        copy.start()
    for copy in copies:
        copy.wait()


def on_device(prior, values, quantity, vertical, lists, alive, taper):
    vmem = pl.BlockSpec(memory_space=pltpu.VMEM)
    smem = pl.BlockSpec(memory_space=pltpu.SMEM)
    dma = pltpu.SemaphoreType.DMA
    peers, chunks = len(ORDER), len(CHUNKS)
    shape = (NV, NCT, MINE, 128)
    prior = prior.reshape(MINE, NV, NCT, 128).transpose(1, 2, 0, 3)
    result = pl.pallas_call(
        kernel,
        out_shape=pltpu.VMEM(shape, prior.dtype),
        in_specs=[pl.BlockSpec(memory_space=pl.ANY)] * 2 + [smem, smem, vmem, vmem, vmem],
        out_specs=pl.BlockSpec(memory_space=pltpu.VMEM),
        scratch_shapes=[
            pltpu.VMEM((NV * NCT, MINE, 128), BF16),
            pltpu.SMEM((PATCHES,), jnp.int32),
            pltpu.VMEM((4, 8, 128), F32),
            pltpu.VMEM((128 * MINE, 128), F32),
            pltpu.VMEM((NV, MEMBERS // MINE, NG, MINE, 128), BF16),
            pltpu.VMEM((NV, MEMBERS // MINE, NG, MINE, 128), BF16),
            pltpu.VMEM((NOT * MINE, 128), F32),
            pltpu.VMEM((4, 8 * MINE, 128), BF16),
            pltpu.VMEM((6, 4, 4, 8 * MINE, 128), BF16),
            pltpu.VMEM((NWT * MEMBERS, 128), F32),
            pltpu.VMEM((NWT, MEMBERS, 128), F32),
            pltpu.VMEM((6, 8, 128), F32),
            pltpu.VMEM((NWT, 2 * MEMBERS, 128), BF16),
            pltpu.VMEM((NWT, 128), F32),
            pltpu.VMEM((PAIRS, MEMBERS, 128), F32),
            pltpu.VMEM((PAIRS, 128), F32),
            pltpu.VMEM((PAIRS, MEMBERS, 128), BF16),
            pltpu.VMEM((NG, 2, MEMBERS, 128), F32),
            pltpu.VMEM((NG, 2, MEMBERS, 128), F32),
            dma,
            dma((chunks, peers)), dma((chunks, peers)), dma((chunks,)),
            dma((12,)), dma((12,)), dma,
            dma((2,)), dma((2,)),
            dma((2,)), dma((2,)), dma,
            dma((chunks, peers)), dma((chunks, peers)), dma((chunks,)),
        ],
        compiler_params=pltpu.CompilerParams(
            collective_id=0, has_side_effects=True, vmem_limit_bytes=54 * 2**20
        ),
    )(
        prior,
        prior.reshape(NV * NCT, MINE, 128),
        quantity * BAND + vertical,
        alive[:, 0],
        values.reshape(4, 8, 128),
        lists,
        taper,
    )
    result = pl.pallas_call(
        keeper,
        out_shape=jax.ShapeDtypeStruct(shape, prior.dtype),
        in_specs=[pl.BlockSpec(memory_space=pltpu.VMEM)],
        out_specs=pl.BlockSpec(memory_space=pl.ANY),
        scratch_shapes=[dma((KEEP,))],
        compiler_params=pltpu.CompilerParams(vmem_limit_bytes=16 * 2**20),
    )(result)
    return result.transpose(2, 0, 1, 3).reshape(MINE, NV, NCT * 128)


def solution(mesh):
    placed = (
        P("mem", None, "lat"),
        P("lat"),
        P("lat"),
        P("lat"),
        P("mem", "lat"),
        P("mem", "lat"),
        P("mem", "lat"),
    )
    return jax.shard_map(
        on_device, mesh=mesh, in_specs=placed, out_specs=P("mem", None, "lat"), check_vma=False
    )
```

```python
import functools
import math

import jax
import jax.numpy as jnp
from jax import lax
from jax.experimental import pallas as pl
from jax.experimental.pallas import tpu as pltpu
from jax.sharding import PartitionSpec as P

MESH = pl.DeviceIdType.MESH
F32, BF16 = jnp.float32, jnp.bfloat16

MEMBERS = 64
MINE = 4
NV = 83
NCT = 64
BAND = NCT * 128
NG = 4
CHUNKS = tuple((NV * i // 8, NV * (i + 1) // 8) for i in range(8))
PATCHES = 32
SLOTS = 512
SPAN = 9
NWT = 48
NOT = 32
NS_STEPS = 8
PAIRS = PATCHES // 2
BATCH = 16

KEEP = 4
FIRST = 2
EARLY = 3

ORDER = (
    (2, 2), (2, 3), (3, 2), (1, 2), (2, 1), (3, 3), (1, 3), (0, 2),
    (3, 1), (1, 1), (2, 0), (0, 3), (0, 1), (3, 0), (1, 0),
)


def dot(a, b):
    return jnp.dot(a, b, preferred_element_type=F32)


def dot_t(a, b):
    return lax.dot_general(a, b, (((1,), (1,)), ((), ())), preferred_element_type=F32)


def halves(value):
    high = value.astype(BF16)
    return high, (value - high.astype(F32)).astype(BF16)


def left(value):
    rows = jnp.concatenate(halves(value), axis=0)
    return jnp.concatenate([rows, rows], axis=1)


def right(value, block_mask):
    high, low = halves(value)
    return jnp.concatenate(
        [
            jnp.concatenate([high, high], axis=0) * block_mask,
            jnp.concatenate([low, low], axis=0) * block_mask,
        ],
        axis=0,
    )


def folded(product):
    half = product.shape[0] // 2
    return product[:half] + product[half:]


def kernel(
    prior, flat, codes, alive, values, lists, taper,
    out,
    mine, tiles, values32, alone, got, made, equiv32, equiv, every, window, perts, value_win, parts, depart,
    gram, proj, weights, wide, wide_out,
    own_sem, in_send, in_recv, in_own, gather_send, gather_recv, gather_own,
    halo_send, halo_recv, value_send, value_recv, value_own, out_send, out_recv, out_own,
):
    me, lat = lax.axis_index("mem"), lax.axis_index("lat")
    bands = lax.axis_size("lat")
    my_y, my_x = me // 4, me % 4
    turn = 1 - 2 * (lat % 2)
    partners = [
        ((my_y + turn * dy + 4) % 4) * 4 + (my_x + turn * dx + 4) % 4 for dx, dy in ORDER
    ]
    north, south = (lat + 1) % bands, (lat + bands - 1) % bands

    load = pltpu.make_async_copy(flat, mine, own_sem)
    load.start()

    barrier = pltpu.get_barrier_semaphore()
    for partner in partners:
        pl.semaphore_signal(barrier, inc=1, device_id=(partner, lat), device_id_type=MESH)
    for band in (north, south):
        pl.semaphore_signal(barrier, inc=1, device_id=(me, band), device_id_type=MESH)
    pl.semaphore_wait(barrier, len(ORDER) + 2)

    def piece(owner, chunk):
        return pl.ds(CHUNKS[chunk][0], CHUNKS[chunk][1] - CHUNKS[chunk][0]), pl.ds(owner * NG, NG)

    def block(owner, chunk):
        return pl.ds(CHUNKS[chunk][0], CHUNKS[chunk][1] - CHUNKS[chunk][0]), owner

    def copies_in(chunk):
        sends = [
            pltpu.make_async_remote_copy(
                src_ref=prior.at[piece(partner, chunk)],
                dst_ref=got.at[block(me, chunk)],
                send_sem=in_send.at[chunk, s],
                recv_sem=in_recv.at[chunk, s],
                device_id=(partner, lat),
                device_id_type=MESH,
            )
            for s, partner in enumerate(partners)
        ]
        own = pltpu.make_async_copy(
            prior.at[piece(me, chunk)], got.at[block(me, chunk)], in_own.at[chunk]
        )
        return sends + [own]

    def copies_out(chunk):
        sends = [
            pltpu.make_async_remote_copy(
                src_ref=made.at[block(partner, chunk)],
                dst_ref=out.at[piece(me, chunk)],
                send_sem=out_send.at[chunk, s],
                recv_sem=out_recv.at[chunk, s],
                device_id=(partner, lat),
                device_id_type=MESH,
            )
            for s, partner in enumerate(partners)
        ]
        own = pltpu.make_async_copy(
            made.at[block(me, chunk)], out.at[piece(me, chunk)], out_own.at[chunk]
        )
        return sends + [own]

    ins = [copies_in(chunk) for chunk in range(len(CHUNKS))]
    outs = [copies_out(chunk) for chunk in range(len(CHUNKS))]
    for chunk in range(FIRST):
        for copy in ins[chunk]:
            copy.start()

    values32[...] = values[...].astype(F32)
    value_copies = [
        pltpu.make_async_remote_copy(
            src_ref=values32.at[source],
            dst_ref=value_win.at[target],
            send_sem=value_send.at[k],
            recv_sem=value_recv.at[k],
            device_id=(me, band),
            device_id_type=MESH,
        )
        for k, (source, target, band) in enumerate(((3, 0, north), (0, 5, south)))
    ]
    value_copies.append(pltpu.make_async_copy(values32, value_win.at[pl.ds(1, 4)], value_own))
    for copy in value_copies:
        copy.start()

    lane4 = lax.broadcasted_iota(jnp.int32, (MINE, 128), 1)
    ones = jnp.ones((8, 128), BF16)

    load.wait()

    def pick(ot, carry):
        for i in range(128):
            code = codes[ot * 128 + i]
            found = mine[lax.shift_right_logical(code, 7)].astype(F32)
            alone[i * MINE : i * MINE + MINE] = jnp.where(lane4 == (code & 127), found, 0.0)
        sorted_rows = [alone[pl.ds(j, 128, stride=MINE), :].astype(BF16) for j in range(MINE)]
        row = dot_t(ones, jnp.concatenate(sorted_rows, axis=0))
        start = (ot // 8) * 8 * MINE + ot % 8
        for j in range(MINE):
            equiv32[pl.ds(start + j * 8, 1), :] = row[0:1, j * 128 : j * 128 + 128]
        return carry

    lax.fori_loop(0, NOT, pick, 0)
    for quarter in range(4):
        equiv[quarter] = equiv32[quarter * 32 : quarter * 32 + 32].astype(BF16)

    side_x = [my_y * 4 + (my_x + d) % 4 for d in (1, 3, 2)]
    side_y = [((my_y + d) % 4) * 4 + my_x for d in (1, 3, 2)]
    first, second = pl.ds(1, 2), pl.ds(3, 2)

    def gather(source, target, k, partner):
        return pltpu.make_async_remote_copy(
            src_ref=source,
            dst_ref=target,
            send_sem=gather_send.at[k],
            recv_sem=gather_recv.at[k],
            device_id=(partner, lat),
            device_id_type=MESH,
        )

    gathers = [
        gather(equiv.at[pl.ds(0, 2)], every.at[first, my_y, my_x], k, partner)
        for k, partner in enumerate(side_x)
    ]
    gathers += [
        gather(equiv.at[pl.ds(2, 2)], every.at[second, my_y, my_x], 3 + k, partner)
        for k, partner in enumerate(side_y)
    ]
    gathers.append(pltpu.make_async_copy(equiv, every.at[pl.ds(1, 4), my_y, my_x], gather_own))
    for copy in gathers:
        copy.start()
    for chunk in range(FIRST, EARLY):
        for copy in ins[chunk]:
            copy.start()
    def first_tile(p, carry):
        tiles[p] = jnp.minimum(lax.shift_right_logical(jnp.min(lists[pl.ds(p, 1), :]), 7), NWT - SPAN)
        return carry

    lax.fori_loop(0, PATCHES, first_tile, 0, unroll=8)

    for copy in gathers:
        copy.wait()
    gathers = [
        gather(every.at[first, my_y], every.at[first, my_y], 6 + k, partner)
        for k, partner in enumerate(side_y)
    ]
    gathers += [
        gather(every.at[second, :, my_x], every.at[second, :, my_x], 9 + k, partner)
        for k, partner in enumerate(side_x)
    ]
    for copy in gathers:
        copy.start()
    for chunk in range(EARLY, len(CHUNKS)):
        for copy in ins[chunk]:
            copy.start()
    for copy in gathers:
        copy.wait()
    halos = [
        pltpu.make_async_remote_copy(
            src_ref=every.at[source],
            dst_ref=every.at[target],
            send_sem=halo_send.at[k],
            recv_sem=halo_recv.at[k],
            device_id=(me, band),
            device_id_type=MESH,
        )
        for k, (source, target, band) in enumerate(((4, 0, north), (1, 5, south)))
    ]
    for copy in halos:
        copy.start()

    def spread_members(q, carry):
        for m in range(MEMBERS // MINE):
            block = every[q, m // 4, m % 4].astype(F32)
            for j in range(MINE):
                start = q * 8 * MEMBERS + m * MINE + j
                window[pl.ds(start, 8, stride=MEMBERS), :] = block[j * 8 : j * 8 + 8]
        return carry

    def center(tile, carry):
        rows = pl.ds(pl.multiple_of(tile * MEMBERS, MEMBERS), MEMBERS)
        field = window[rows, :]
        mean = jnp.sum(field, axis=0, keepdims=True) * (1.0 / MEMBERS)
        pert = field - mean
        perts[tile] = pert
        parts[tile] = jnp.concatenate(halves(pert), axis=0)
        depart[pl.ds(tile, 1), :] = value_win[tile // 8, pl.ds(tile % 8, 1), :] - mean
        return carry

    for copy in value_copies:
        copy.wait()
    lax.fori_loop(1, 5, spread_members, 0)
    lax.fori_loop(8, 40, center, 0)
    for copy in halos:
        copy.wait()
    for quarter in (0, 5):
        spread_members(quarter, 0)
        lax.fori_loop(quarter * 8, quarter * 8 + 8, center, 0)

    slot = lax.broadcasted_iota(jnp.int32, (1, SLOTS), 1)
    high_row = lax.broadcasted_iota(jnp.int32, (16, SLOTS), 0)
    low_row = lax.broadcasted_iota(jnp.int32, (128, SLOTS), 0)
    lane64 = lax.broadcasted_iota(jnp.int32, (MEMBERS, 128), 1)
    row64 = lax.broadcasted_iota(jnp.int32, (MEMBERS, 128), 0)
    first_half = lane64 < MEMBERS
    diagonal = (lane64 % MEMBERS) == row64
    unit = diagonal.astype(F32)
    first_lane = lax.broadcasted_iota(jnp.int32, (1, 128), 1) < MEMBERS

    def one_patch(p):
        base = tiles[p]
        place = lists[pl.ds(p, 1), :] - base * 128
        weight = jnp.where(slot < alive[p], taper[pl.ds(p, 1), :], 0.0)
        hit = high_row == lax.shift_right_arithmetic(place, 7)
        laid = []
        rest = weight
        for _ in range(3):
            part = rest.astype(BF16).astype(F32)
            laid.append(jnp.where(hit, part, 0.0))
            rest = rest - part
        laid = jnp.concatenate(laid, axis=0).astype(BF16)
        lows = jnp.where(low_row == (place & 127), 1.0, 0.0).astype(BF16)
        laid = dot_t(laid, lows)
        laid = laid[0:16] + laid[16:32] + laid[32:48]
        lefts, rights = [], []
        for t in range(SPAN):
            w = laid[t : t + 1]
            tile = base + t
            high, low = halves(perts[tile] * w)
            d_high, d_low = halves(depart[pl.ds(tile, 1), :] * w)
            ends = jnp.concatenate(
                [d_high.astype(F32), d_low.astype(F32), jnp.zeros((14, 128), F32)], axis=0
            )
            lefts.append(jnp.concatenate([high, low, ends.astype(BF16)], axis=0))
            rights.append(parts[tile])
        product = dot_t(jnp.concatenate(lefts, axis=1), jnp.concatenate(rights, axis=1))
        return product

    def fold_first(a, b):
        return a + pltpu.roll(a, MEMBERS, 1) + b

    def fold_second(a, b):
        return a + pltpu.roll(a, MEMBERS, 1) + pltpu.roll(b, MEMBERS, 1)

    def one_pair(k, carry):
        one, two = one_patch(2 * k), one_patch(2 * k + 1)
        both = jnp.where(
            first_half,
            fold_first(one[0:64], one[64:128]),
            fold_second(two[0:64], two[64:128]),
        )
        gram[k] = both + (MEMBERS - 1.0) * unit
        row_one, row_two = one[128:136], two[128:136]
        swapped_one, swapped_two = pltpu.roll(row_one, MEMBERS, 1), pltpu.roll(row_two, MEMBERS, 1)
        end_one = row_one[0:1] + swapped_one[0:1] + row_one[1:2]
        end_two = row_two[0:1] + swapped_two[0:1] + swapped_two[1:2]
        proj[pl.ds(k, 1), :] = jnp.where(first_lane, end_one, end_two)
        return carry

    lax.fori_loop(0, PAIRS, one_pair, 0)

    row128 = lax.broadcasted_iota(jnp.int32, (128, 128), 0)
    lane128 = lax.broadcasted_iota(jnp.int32, (128, 128), 1)
    block_mask = jnp.where((row128 < MEMBERS) == (lane128 < MEMBERS), 1.0, 0.0).astype(BF16)

    def half_sums(value):
        one = jnp.sum(jnp.where(lane64[: value.shape[0]] < MEMBERS, value, 0.0), axis=1, keepdims=True)
        two = jnp.sum(jnp.where(lane64[: value.shape[0]] < MEMBERS, 0.0, value), axis=1, keepdims=True)
        return jnp.where(lane64[: value.shape[0]] < MEMBERS, one, two)

    def batch_of_pairs(batch, carry):
        pairs = [batch * BATCH + i for i in range(BATCH)]
        grams = [gram[k] for k in pairs]
        traces = []
        for g in grams:
            diag = jnp.sum(jnp.where(diagonal, g, 0.0), axis=0, keepdims=True)
            one = jnp.sum(jnp.where(first_lane, diag, 0.0), axis=1, keepdims=True)
            two = jnp.sum(jnp.where(first_lane, 0.0, diag), axis=1, keepdims=True)
            traces.append(jnp.where(first_lane, one, two))
        roots = [g / t for g, t in zip(grams, traces)]
        mids = [1.5 * unit - 0.5 * r for r in roots]
        roots = [folded(dot(left(r), right(m, block_mask))) for r, m in zip(roots, mids)]
        invs = mids

        def sweep(_, state):
            roots, invs = state
            mids = [
                1.5 * unit - 0.5 * folded(dot(left(v), right(r, block_mask)))
                for r, v in zip(roots, invs)
            ]
            new_roots, new_invs = [], []
            for r, v, m in zip(roots, invs, mids):
                both = dot(jnp.concatenate([left(r), left(v)], axis=0), right(m, block_mask))
                new_roots.append(folded(both[0:128]))
                new_invs.append(folded(both[128:256]))
            return new_roots, new_invs

        roots, invs = lax.fori_loop(0, NS_STEPS - 2, sweep, (roots, invs))
        mids = [
            1.5 * unit - 0.5 * folded(dot(left(v), right(r, block_mask)))
            for r, v in zip(roots, invs)
        ]
        invs = [folded(dot(left(v), right(m, block_mask))) for v, m in zip(invs, mids)]

        for k, v, t in zip(pairs, invs, traces):
            factor = right(v, block_mask)
            row = proj[pl.ds(k, 1), :]
            for _ in range(2):
                wide_row = jnp.concatenate([row, jnp.zeros((7, 128), F32)], axis=0)
                row = folded(dot(left(wide_row), factor))[0:1]
            full = v * (math.sqrt(MEMBERS - 1.0) * lax.rsqrt(t)) + row / t
            full = full + (1.0 - half_sums(full)) * (1.0 / MEMBERS)
            weights[k] = full.astype(BF16)
        return carry

    lax.fori_loop(0, PAIRS // BATCH, batch_of_pairs, 0)

    lane_patch = lax.broadcasted_iota(jnp.int32, (MEMBERS, 128), 1) // 16
    masks = [jnp.where(lane_patch == p, 1.0, 0.0).astype(BF16) for p in range(8)]
    factors = [
        jnp.concatenate([weights[group * 4 + i] for i in range(4)], axis=1) for group in range(NG)
    ]

    def some(first, count):
        for group in range(NG):
            for i in range(count):
                for m in range(MEMBERS // MINE):
                    wide[group, i, m * MINE : m * MINE + MINE] = got[first + i, m, group].astype(F32)
        for group in range(NG):
            fields = []
            for i in range(count):
                field = wide[group, i].astype(BF16)
                fields.append(jnp.concatenate([field * m for m in masks], axis=0))
            result = dot(factors[group], jnp.concatenate(fields, axis=1))
            for i in range(count):
                wide_out[group, i] = result[:, i * 128 : i * 128 + 128]
        for group in range(NG):
            for i in range(count):
                for m in range(MEMBERS // MINE):
                    made[first + i, m, group] = wide_out[
                        group, i, m * MINE : m * MINE + MINE
                    ].astype(BF16)

    for chunk, (start, stop) in enumerate(CHUNKS):
        for copy in ins[chunk]:
            copy.wait()

        def variables(step, carry, start=start):
            some(start + step * 2, 2)
            return carry

        lax.fori_loop(0, (stop - start) // 2, variables, 0)
        if (stop - start) % 2:
            some(stop - 1, 1)
        for copy in outs[chunk]:
            copy.start()
    for chunk in range(len(CHUNKS)):
        for copy in outs[chunk]:
            copy.wait()


def keeper(made, out, writes):
    bounds = [NV * i // KEEP for i in range(KEEP + 1)]
    copies = [
        pltpu.make_async_copy(
            made.at[pl.ds(start, stop - start)], out.at[pl.ds(start, stop - start)], writes.at[k]
        )
        for k, (start, stop) in enumerate(zip(bounds, bounds[1:]))
    ]
    for copy in copies:
        copy.start()
    for copy in copies:
        copy.wait()


def on_device(prior, values, quantity, vertical, lists, alive, taper):
    vmem = pl.BlockSpec(memory_space=pltpu.VMEM)
    smem = pl.BlockSpec(memory_space=pltpu.SMEM)
    dma = pltpu.SemaphoreType.DMA
    peers, chunks = len(ORDER), len(CHUNKS)
    shape = (NV, NCT, MINE, 128)
    prior = prior.reshape(MINE, NV, NCT, 128).transpose(1, 2, 0, 3)
    result = pl.pallas_call(
        kernel,
        out_shape=pltpu.VMEM(shape, prior.dtype),
        in_specs=[pl.BlockSpec(memory_space=pl.ANY)] * 2 + [smem, smem, vmem, vmem, vmem],
        out_specs=pl.BlockSpec(memory_space=pltpu.VMEM),
        scratch_shapes=[
            pltpu.VMEM((NV * NCT, MINE, 128), BF16),
            pltpu.SMEM((PATCHES,), jnp.int32),
            pltpu.VMEM((4, 8, 128), F32),
            pltpu.VMEM((128 * MINE, 128), F32),
            pltpu.VMEM((NV, MEMBERS // MINE, NG, MINE, 128), BF16),
            pltpu.VMEM((NV, MEMBERS // MINE, NG, MINE, 128), BF16),
            pltpu.VMEM((NOT * MINE, 128), F32),
            pltpu.VMEM((4, 8 * MINE, 128), BF16),
            pltpu.VMEM((6, 4, 4, 8 * MINE, 128), BF16),
            pltpu.VMEM((NWT * MEMBERS, 128), F32),
            pltpu.VMEM((NWT, MEMBERS, 128), F32),
            pltpu.VMEM((6, 8, 128), F32),
            pltpu.VMEM((NWT, 2 * MEMBERS, 128), BF16),
            pltpu.VMEM((NWT, 128), F32),
            pltpu.VMEM((PAIRS, MEMBERS, 128), F32),
            pltpu.VMEM((PAIRS, 128), F32),
            pltpu.VMEM((PAIRS, MEMBERS, 128), BF16),
            pltpu.VMEM((NG, 2, MEMBERS, 128), F32),
            pltpu.VMEM((NG, 2, MEMBERS, 128), F32),
            dma,
            dma((chunks, peers)), dma((chunks, peers)), dma((chunks,)),
            dma((12,)), dma((12,)), dma,
            dma((2,)), dma((2,)),
            dma((2,)), dma((2,)), dma,
            dma((chunks, peers)), dma((chunks, peers)), dma((chunks,)),
        ],
        compiler_params=pltpu.CompilerParams(
            collective_id=0, has_side_effects=True, vmem_limit_bytes=54 * 2**20
        ),
    )(
        prior,
        prior.reshape(NV * NCT, MINE, 128),
        quantity * BAND + vertical,
        alive[:, 0],
        values.reshape(4, 8, 128),
        lists,
        taper,
    )
    result = pl.pallas_call(
        keeper,
        out_shape=jax.ShapeDtypeStruct(shape, prior.dtype),
        in_specs=[pl.BlockSpec(memory_space=pltpu.VMEM)],
        out_specs=pl.BlockSpec(memory_space=pl.ANY),
        scratch_shapes=[dma((KEEP,))],
        compiler_params=pltpu.CompilerParams(vmem_limit_bytes=16 * 2**20),
    )(result)
    return result.transpose(2, 0, 1, 3).reshape(MINE, NV, NCT * 128)


def solution(mesh):
    placed = (
        P("mem", None, "lat"),
        P("lat"),
        P("lat"),
        P("lat"),
        P("mem", "lat"),
        P("mem", "lat"),
        P("mem", "lat"),
    )
    return jax.shard_map(
        on_device, mesh=mesh, in_specs=placed, out_specs=P("mem", None, "lat"), check_vma=False
    )
```
